32 devices in a mesh: seg: 16 (over z, x, core), band: 2 (over y).
Axes of the slice: x: 2, y: 2, z: 4, core: 2. Of those that a mesh axis runs over, the one named last changes fastest.
Arguments:
- spectra: bfloat16 [2, 16384, 1024], P(None, 'seg', 'band'), may hold values from -100 to 100, as said below
- pair_first: int32 [65536], P('seg'), may hold values from 0 to 16383, as said below
- pair_second: int32 [65536], P('seg'), may hold values from 0 to 16383, as said below
- pair_bin: int32 [65536], P('seg'), may hold values from 0 to 127, as said below
Outputs:
- correlation_stack: float32 [128, 1024], P('seg', 'band')
The draws below stay inside these ranges and needn't reach their ends.
Inputs may be any that keep to these rules, and one draw needn't show every extreme that they name: The spectra are finite; their magnitude varies from channel to channel and from bin to bin. `pair_first`: rows s * 4096 to (s + 1) * 4096 - 1 name channels of segment s, that is s * 1024 to (s + 1) * 1024 - 1. pair_second differs from pair_first of the same row by 1 to 256 in either direction; some row of every segment differs by exactly 256. `pair_bin`: offset bins s * 8 to (s + 1) * 8 - 1 belong to segment s; of one segment's rows at most 256 have bins of any one segment, and in every draw the bins of some segment receive exactly 256 rows from every segment.
All inputs are finite; a program needn't handle non-finite values.
Results may differ from the reference program's by a relative error of at most 0.0054.
Values may be sent and summed in bfloat16 or wider, within the bound.
A program may use at most 64 MiB of HBM per device.

```python
import math
import jax
import jax.numpy as jnp
from jax import lax

CH_DEV = 1024
PAIRS_DEV = 4096
OB_DEV = 8
REACH = 256
FREQ = 1024
LAGS = 1024
HALF_WIN = 64
CAP = 256
CHANNELS = 16384
NPAIRS = 65536
OBINS = 128
N_SEG = 16


def draw_spectra(key, part):
    bins_frac = jnp.arange(FREQ, dtype=jnp.float32)[None, :] / FREQ
    amplitude = jax.random.uniform(jax.random.fold_in(key, 1), (CHANNELS, 1), minval=0.5, maxval=1.2)
    cycles = jax.random.uniform(jax.random.fold_in(key, 2), (CHANNELS, 1), minval=1.0, maxval=3.0)
    offset_phase = jax.random.uniform(jax.random.fold_in(key, 3), (CHANNELS, 1), minval=0.0, maxval=6.283)
    envelope = jnp.exp(amplitude * jnp.sin(6.2832 * cycles * bins_frac + offset_phase))
    roughness = jnp.exp(jax.random.uniform(jax.random.fold_in(key, 4), (CHANNELS, FREQ), maxval=math.log(3.0)))
    noise_part = jax.random.truncated_normal(jax.random.fold_in(key, 5), -4.0, 4.0, (2, CHANNELS, FREQ))
    values = noise_part * (envelope * roughness)[None]
    return values.astype(jnp.bfloat16)


def pair_channels(key):
    row_index = jnp.arange(NPAIRS, dtype=jnp.int32)
    segment_of = row_index // PAIRS_DEV
    within = jax.random.randint(jax.random.fold_in(key, 11), (NPAIRS,), 0, CH_DEV)
    firsts = segment_of * CH_DEV + within
    distance = jax.random.randint(jax.random.fold_in(key, 12), (NPAIRS,), 1, REACH + 1)
    distance = jnp.where(row_index % PAIRS_DEV == 0, REACH, distance)
    direction = 2 * jax.random.randint(jax.random.fold_in(key, 13), (NPAIRS,), 0, 2) - 1
    seconds = firsts + direction * distance
    outside = (seconds < 0) | (seconds >= CHANNELS)
    seconds = jnp.where(outside, firsts - direction * distance, seconds)
    return (firsts.astype(jnp.int32), seconds.astype(jnp.int32))


def draw_pair_first(key, part):
    return pair_channels(key)[0]


def draw_pair_second(key, part):
    return pair_channels(key)[1]


def draw_pair_bin(key, part):
    segments = NPAIRS // PAIRS_DEV
    hottest = jax.random.randint(jax.random.fold_in(key, 21), (), 0, segments)
    row_rank = jnp.arange(PAIRS_DEV, dtype=jnp.int32)
    spread_owner = (hottest + 1 + (row_rank - CAP) % (segments - 1)) % segments
    owner_list = jnp.where(row_rank < CAP, hottest, spread_owner)

    def one_block(block_key):
        return owner_list[jax.random.permutation(block_key, PAIRS_DEV)]
    block_keys = jax.random.split(jax.random.fold_in(key, 22), segments)
    owners_all = jax.vmap(one_block)(block_keys).reshape(-1)
    local_bin = jax.random.randint(jax.random.fold_in(key, 23), (NPAIRS,), 0, OB_DEV)
    return (owners_all * OB_DEV + local_bin).astype(jnp.int32)


def setup_inputs(seed: int = 0) -> dict:
    seeds = jax.random.split(jax.random.key(seed), 5)
    return {
        "spectra": draw_spectra(jax.random.fold_in(seeds[4], 71), 0),
        "pair_first": draw_pair_first(jax.random.fold_in(seeds[4], 71), 0),
        "pair_second": draw_pair_second(jax.random.fold_in(seeds[4], 71), 0),
        "pair_bin": draw_pair_bin(jax.random.fold_in(seeds[4], 71), 0),
    }


epsilon = 1e-06

def lag_table(first_bin, local_bins, total_bins, lag_count):
    frequency = first_bin + jnp.arange(local_bins, dtype=jnp.int32)
    lag_index = jnp.arange(lag_count, dtype=jnp.int32) - lag_count // 2
    residue = frequency[:, None] * lag_index[None, :] % (2 * total_bins)
    angles = residue.astype(jnp.float32) * (math.pi / total_bins)
    cosine = jnp.cos(angles) / total_bins
    negsine = -jnp.sin(angles) / total_bins
    return jnp.concatenate([cosine, negsine], axis=0).astype(jnp.bfloat16)

def reference(spectra, pair_first, pair_second, pair_bin):
    real_part = spectra[0].astype(jnp.float32)
    imag_part = spectra[1].astype(jnp.float32)
    power_sum = real_part * real_part + imag_part * imag_part
    window_sum = lax.reduce_window(power_sum, jnp.zeros((), power_sum.dtype), lax.add, (1, 2 * HALF_WIN + 1), (1, 1), ((0, 0), (HALF_WIN, HALF_WIN)))
    scaling = lax.rsqrt(window_sum / (2 * HALF_WIN + 1) + epsilon)
    white_real = (real_part * scaling).astype(jnp.bfloat16)
    white_imag = (imag_part * scaling).astype(jnp.bfloat16)
    table = lag_table(0, FREQ, FREQ, LAGS).astype(jnp.float32)

    def add_block(running, block_data):
        firsts, seconds, bin_ids = block_data
        first_real = white_real[firsts].astype(jnp.float32)
        first_imag = white_imag[firsts].astype(jnp.float32)
        second_real = white_real[seconds].astype(jnp.float32)
        second_imag = white_imag[seconds].astype(jnp.float32)
        cross_real = first_real * second_real + first_imag * second_imag
        cross_imag = first_imag * second_real - first_real * second_imag
        cross_both = jnp.concatenate([cross_real, cross_imag], axis=1).astype(jnp.bfloat16)
        cross_both = lax.optimization_barrier(cross_both).astype(jnp.float32)
        return (running + jax.ops.segment_sum(cross_both, bin_ids, num_segments=OBINS), None)
    blocks = (pair_first.reshape(N_SEG, PAIRS_DEV), pair_second.reshape(N_SEG, PAIRS_DEV), pair_bin.reshape(N_SEG, PAIRS_DEV))
    stacked, _ = lax.scan(add_block, jnp.zeros((OBINS, 2 * FREQ), jnp.float32), blocks)
    return jnp.dot(stacked, table, precision=lax.Precision.HIGHEST)
```

```python
import functools
import math

import jax
import jax.numpy as jnp
from jax import lax
from jax.experimental import pallas as pl
from jax.experimental.pallas import tpu as pltpu
from jax.sharding import PartitionSpec as P

OB_DEV = 8
REACH = 256
FREQ = 1024
LAGS = 1024
HALF_WIN = 64
BANKS = 4
LANES = 128
FINE = 32
NEAR_SEGS = 4
MESH = pl.DeviceIdType.MESH

epsilon = 1e-06


def extended(block, sides, width):
    for axis, dim in sides:
        count = lax.axis_size(axis)
        forward = [(i, i + 1) for i in range(count - 1)]
        backward = [(target, source) for source, target in forward]
        low = lax.ppermute(
            lax.slice_in_dim(block, block.shape[dim] - width, None, axis=dim), axis, forward
        )
        high = lax.ppermute(lax.slice_in_dim(block, 0, width, axis=dim), axis, backward)
        block = jnp.concatenate([low, block, high], axis=dim)
    return block


def window_matrix(local_bins, half_width):
    padded_index = jnp.arange(local_bins + 2 * half_width)[:, None]
    bin_index = jnp.arange(local_bins)[None, :]
    inside = (padded_index >= bin_index) & (padded_index <= bin_index + 2 * half_width)
    return inside.astype(jnp.float32)


def circle(first, step, count):
    rows = lax.broadcasted_iota(jnp.int32, (count, LAGS), 0) * step + first
    lags = lax.broadcasted_iota(jnp.int32, (count, LAGS), 1) - LAGS // 2
    residue = jnp.bitwise_and(rows * lags, 2 * FREQ - 1)
    residue = residue - jnp.where(residue >= FREQ, 2 * FREQ, 0)
    angles = residue.astype(jnp.float32) * (math.pi / FREQ)
    return jnp.cos(angles), jnp.sin(angles)


def write_basis(first_bin, local_bins, table):
    coarse_cos, coarse_sin = circle(first_bin, FINE, local_bins // FINE)
    fine_cos, fine_sin = circle(0, 1, FINE)
    fine_cos, fine_sin = fine_cos * (1.0 / FREQ), fine_sin * (1.0 / FREQ)
    for i in range(local_bins // FINE):
        cc, cs = coarse_cos[i : i + 1], coarse_sin[i : i + 1]
        table[i * FINE : (i + 1) * FINE, :] = (cc * fine_cos - cs * fine_sin).astype(jnp.bfloat16)
        table[local_bins + i * FINE : local_bins + (i + 1) * FINE, :] = (
            -(cs * fine_cos + cc * fine_sin)
        ).astype(jnp.bfloat16)


def pair_kernel(
    local_bins, bins, first_ref, second_ref, bin_ref, white_ref, out_ref, rows, table, *banks
):
    parts = 2 * local_bins // LANES
    half = parts // 2
    channels = white_ref.shape[0]
    write_basis(lax.axis_index("band") * local_bins, local_bins, table)
    for bank in banks:
        bank[...] = jnp.zeros_like(bank)
    for j in range(parts):
        rows[pl.ds(j, channels, stride=parts), :] = white_ref[
            :, j * LANES : (j + 1) * LANES
        ].astype(jnp.float32)

    def group(step, carry):
        base = step * BANKS
        updates = []
        for k, bank in enumerate(banks):
            a = pl.multiple_of(first_ref[base + k], parts)
            b = pl.multiple_of(second_ref[base + k], parts)
            o = pl.multiple_of(bin_ref[base + k], 2 * parts)
            first = rows[pl.ds(a, parts), :]
            second = rows[pl.ds(b, parts), :]
            straight = bank[pl.ds(o, parts), :] + first * second
            crossed = bank[pl.ds(o + parts, parts), :] + pltpu.roll(first, half, 0) * second
            updates.append((bank, o, straight, crossed))
        for bank, o, straight, crossed in updates:
            bank[pl.ds(o, parts), :] = straight
            bank[pl.ds(o + parts, parts), :] = crossed
        return carry

    lax.fori_loop(0, first_ref.shape[0] // BANKS, group, 0, unroll=4)

    def stacked(j):
        total = banks[0][pl.ds(j, bins, stride=2 * parts), :]
        for bank in banks[1:]:
            total = total + bank[pl.ds(j, bins, stride=2 * parts), :]
        return total

    lags = jnp.zeros((bins, LAGS), jnp.float32)
    for j in range(parts):
        if j < half:
            piece = stacked(j) + stacked(half + j)
        else:
            piece = stacked(parts + j - half) - stacked(parts + j)
        high = piece.astype(jnp.bfloat16)
        low = (piece - high.astype(jnp.float32)).astype(jnp.bfloat16)
        basis = table[j * LANES : (j + 1) * LANES, :]
        lags += jnp.dot(high, basis, preferred_element_type=jnp.float32)
        lags += jnp.dot(low, basis, preferred_element_type=jnp.float32)
    out_ref[...] = lags


def sum_kernel(segments, bands, lags_ref, out_ref, send, near, mid, far, s1, r1, s2, r2):
    near_count = NEAR_SEGS * bands
    far_count = segments // NEAR_SEGS
    width = LAGS // bands
    seg, band = lax.axis_index("seg"), lax.axis_index("band")
    row, col = seg // NEAR_SEGS, seg % NEAR_SEGS
    me = col * bands + band

    def near_peer(d):
        p = lax.rem(me + d, near_count)
        return p, (row * NEAR_SEGS + p // bands, lax.rem(p, bands))

    def far_peer(d):
        p = lax.rem(row + d, far_count)
        return p, (p * NEAR_SEGS + col, band)

    barrier = pltpu.get_barrier_semaphore()
    for d in range(1, near_count):
        pl.semaphore_signal(barrier, inc=1, device_id=near_peer(d)[1], device_id_type=MESH)
    for d in range(1, far_count):
        pl.semaphore_signal(barrier, inc=1, device_id=far_peer(d)[1], device_id_type=MESH)
    for p in range(near_count):
        c, b = p // bands, p % bands
        block = [
            lags_ref[
                (r * NEAR_SEGS + c) * OB_DEV : (r * NEAR_SEGS + c + 1) * OB_DEV,
                b * width : (b + 1) * width,
            ]
            for r in range(far_count)
        ]
        send[p] = jnp.concatenate(block, axis=0).astype(jnp.bfloat16)
    pl.semaphore_wait(barrier, near_count - 1 + far_count - 1)

    def near_copy(d):
        p, device = near_peer(d)
        return pltpu.make_async_remote_copy(
            src_ref=send.at[p], dst_ref=near.at[d], send_sem=s1.at[d], recv_sem=r1.at[d],
            device_id=device, device_id_type=MESH,
        )

    def far_copy(d):
        p, device = far_peer(d)
        return pltpu.make_async_remote_copy(
            src_ref=mid.at[p], dst_ref=far.at[d], send_sem=s2.at[d], recv_sem=r2.at[d],
            device_id=device, device_id_type=MESH,
        )

    for d in range(1, near_count):
        near_copy(d).start()
    total = send[me].astype(jnp.float32)
    for d in range(1, near_count):
        near_copy(d).wait_recv()
        total += near[d].astype(jnp.float32)
    for r in range(far_count):
        mid[r] = total[r * OB_DEV : (r + 1) * OB_DEV]
    for d in range(1, far_count):
        far_copy(d).start()
    result = mid[row]
    for d in range(1, far_count):
        far_copy(d).wait_recv()
        result += far[d]
    out_ref[...] = result
    for d in range(1, near_count):
        near_copy(d).wait_send()
    for d in range(1, far_count):
        far_copy(d).wait_send()


def stack_pairs(white, first, second, bins_at, local_bins, bins):
    parts = 2 * local_bins // LANES
    smem = pl.BlockSpec(memory_space=pltpu.SMEM)
    vmem = pl.BlockSpec(memory_space=pltpu.VMEM)
    return pl.pallas_call(
        functools.partial(pair_kernel, local_bins, bins),
        out_shape=jax.ShapeDtypeStruct((bins, LAGS), jnp.float32),
        in_specs=[smem, smem, smem, vmem],
        out_specs=vmem,
        scratch_shapes=[
            pltpu.VMEM((white.shape[0] * parts, LANES), jnp.float32),
            pltpu.VMEM((2 * local_bins, LAGS), jnp.bfloat16),
        ]
        + [pltpu.VMEM((bins * 2 * parts, LANES), jnp.float32)] * BANKS,
        compiler_params=pltpu.CompilerParams(vmem_limit_bytes=48 * 2**20),
        name="pairs",
    )(first, second, bins_at, white)


def sum_lags(lags, segments, bands):
    near_count, far_count = NEAR_SEGS * bands, segments // NEAR_SEGS
    width = LAGS // bands
    vmem = pl.BlockSpec(memory_space=pltpu.VMEM)
    dma = pltpu.SemaphoreType.DMA
    return pl.pallas_call(
        functools.partial(sum_kernel, segments, bands),
        out_shape=jax.ShapeDtypeStruct((OB_DEV, width), jnp.float32),
        in_specs=[vmem],
        out_specs=vmem,
        scratch_shapes=[
            pltpu.VMEM((near_count, far_count * OB_DEV, width), jnp.bfloat16),
            pltpu.VMEM((near_count, far_count * OB_DEV, width), jnp.bfloat16),
            pltpu.VMEM((far_count, OB_DEV, width), jnp.float32),
            pltpu.VMEM((far_count, OB_DEV, width), jnp.float32),
            dma((near_count,)), dma((near_count,)), dma((far_count,)), dma((far_count,)),
        ],
        compiler_params=pltpu.CompilerParams(
            collective_id=1, has_side_effects=True, vmem_limit_bytes=32 * 2**20
        ),
        name="sums",
    )(lags)


def per_device(spectra, pair_first, pair_second, pair_bin):
    seg_position = lax.axis_index("seg")
    segments = lax.axis_size("seg")
    bands = lax.axis_size("band")
    channels = spectra.shape[1]
    local_bins = spectra.shape[2]
    parts = 2 * local_bins // LANES
    real_part = spectra[0].astype(jnp.float32)
    imag_part = spectra[1].astype(jnp.float32)
    power_sum = real_part * real_part + imag_part * imag_part
    padded_power = extended(power_sum, (("band", 1),), HALF_WIN)
    window_sum = jnp.dot(
        padded_power, window_matrix(local_bins, HALF_WIN), precision=lax.Precision.HIGHEST
    )
    scaling = lax.rsqrt(window_sum / (2 * HALF_WIN + 1) + epsilon)
    whitened = jnp.concatenate([real_part * scaling, imag_part * scaling], axis=1).astype(
        jnp.bfloat16
    )
    near_rows = extended(whitened, (("seg", 0),), REACH)
    shift = REACH - seg_position * channels
    lags = stack_pairs(
        near_rows,
        (pair_first + shift) * parts,
        (pair_second + shift) * parts,
        pair_bin * (2 * parts),
        local_bins,
        segments * OB_DEV,
    )
    return sum_lags(lags, segments, bands)


def solution(mesh):
    placed = (P(None, "seg", "band"), P("seg"), P("seg"), P("seg"))
    return jax.shard_map(
        per_device, mesh=mesh, in_specs=placed, out_specs=P("seg", "band"), check_vma=False
    )
```

```python
import functools
import math

import jax
import jax.numpy as jnp
from jax import lax
from jax.experimental import pallas as pl
from jax.experimental.pallas import tpu as pltpu
from jax.sharding import PartitionSpec as P

OB_DEV = 8
REACH = 256
FREQ = 1024
LAGS = 1024
HALF_WIN = 64
BANKS = 4
LANES = 128
FINE = 32
NEAR_SEGS = 4
MESH = pl.DeviceIdType.MESH

epsilon = 1e-06


def circle(first, step, count):
    rows = lax.broadcasted_iota(jnp.int32, (count, LAGS), 0) * step + first
    lags = lax.broadcasted_iota(jnp.int32, (count, LAGS), 1) - LAGS // 2
    residue = jnp.bitwise_and(rows * lags, 2 * FREQ - 1)
    residue = residue - jnp.where(residue >= FREQ, 2 * FREQ, 0)
    angles = residue.astype(jnp.float32) * (math.pi / FREQ)
    return jnp.cos(angles), jnp.sin(angles)


def write_basis(first_bin, local_bins, table):
    coarse_cos, coarse_sin = circle(first_bin, FINE, local_bins // FINE)
    fine_cos, fine_sin = circle(0, 1, FINE)
    fine_cos, fine_sin = fine_cos * (1.0 / FREQ), fine_sin * (1.0 / FREQ)
    for i in range(local_bins // FINE):
        cc, cs = coarse_cos[i : i + 1], coarse_sin[i : i + 1]
        table[i * FINE : (i + 1) * FINE, :] = (cc * fine_cos - cs * fine_sin).astype(jnp.bfloat16)
        table[local_bins + i * FINE : local_bins + (i + 1) * FINE, :] = (
            -(cs * fine_cos + cc * fine_sin)
        ).astype(jnp.bfloat16)


def whiten_kernel(
    segments, bands, spectra_ref, first_ref, second_ref, bin_ref,
    rows, table, first_out, second_out, bin_out,
    near, window, edge_out, left_in, right_in, load_sem, send_sem, recv_sem,
):
    channels, local_bins = spectra_ref.shape[1:]
    groups = channels // REACH
    parts = 2 * local_bins // LANES
    half = parts // 2
    packed = REACH // 2
    seg, band = lax.axis_index("seg"), lax.axis_index("band")

    seg_there = {-1: seg > 0, 0: None, 1: seg < segments - 1}
    band_there = {-1: band > 0, 0: None, 1: band < bands - 1}
    peers = [(ds, db) for ds in (-1, 0, 1) for db in (-1, 0, 1) if (ds, db) != (0, 0)]

    def there(ds, db):
        if ds == 0:
            return band_there[db]
        if db == 0:
            return seg_there[ds]
        return jnp.logical_and(seg_there[ds], band_there[db])

    load = pltpu.make_async_copy(
        spectra_ref, near.at[:, pl.ds(REACH, channels), :], load_sem.at[0]
    )
    load.start()
    barrier = pltpu.get_barrier_semaphore()
    for ds, db in peers:
        @pl.when(there(ds, db))
        def _():
            pl.semaphore_signal(
                barrier, inc=1, device_id=(seg + ds, band + db), device_id_type=MESH
            )
    seg_span = 3 - jnp.where(seg == 0, 1, 0) - jnp.where(seg == segments - 1, 1, 0)
    band_span = 3 - jnp.where(band == 0, 1, 0) - jnp.where(band == bands - 1, 1, 0)
    pl.semaphore_wait(barrier, seg_span * band_span - 1)

    def sending(ds, db):
        slot = peers.index((ds, db))
        if db == 0:
            source = spectra_ref.at[:, pl.ds(channels - REACH if ds > 0 else 0, REACH), :]
            target = near.at[:, pl.ds(0 if ds > 0 else REACH + channels, REACH), :]
        else:
            side, box = (1, left_in) if db > 0 else (0, right_in)
            if ds == 0:
                source = edge_out.at[side]
                target = box.at[pl.ds(1, groups)]
            else:
                source = edge_out.at[side, pl.ds(groups - 1 if ds > 0 else 0, 1)]
                target = box.at[pl.ds(0 if ds > 0 else groups + 1, 1)]
        return pltpu.make_async_remote_copy(
            src_ref=source, dst_ref=target, send_sem=send_sem.at[slot],
            recv_sem=recv_sem.at[slot], device_id=(seg + ds, band + db), device_id_type=MESH,
        )

    def start(ds, db):
        @pl.when(there(ds, db))
        def _():
            sending(ds, db).start()

    def arrived(ds, db):
        @pl.when(there(-ds, -db))
        def _():
            sending(ds, db).wait_recv()

    start(-1, 0)
    start(1, 0)
    load.wait()

    lane = lax.broadcasted_iota(jnp.int32, (packed, LANES), 1)

    def edge(side, group):
        at = 0 if side == 0 else local_bins - LANES
        real = near[0, pl.ds(REACH + group * REACH, REACH), at : at + LANES].astype(jnp.float32)
        imag = near[1, pl.ds(REACH + group * REACH, REACH), at : at + LANES].astype(jnp.float32)
        power = real * real + imag * imag
        upper, lower = power[:packed], power[packed:]
        if side == 0:
            both = jnp.where(lane < HALF_WIN, upper, pltpu.roll(lower, HALF_WIN, 1))
        else:
            both = jnp.where(lane < HALF_WIN, pltpu.roll(upper, HALF_WIN, 1), lower)
        edge_out[side, group] = both.astype(jnp.bfloat16)

    for side, db in ((0, -1), (1, 1)):
        @pl.when(band_there[db])
        def _():
            for group in range(groups):
                edge(side, group)
        start(0, db)
        start(-1, db)
        start(1, db)
    for db, box in ((-1, left_in), (1, right_in)):
        @pl.when(jnp.logical_not(band_there[db]))
        def _():
            box[...] = jnp.zeros_like(box)

    shift = REACH - seg * channels
    first_out[...] = (first_ref[...] + shift) * parts
    second_out[...] = (second_ref[...] + shift) * parts
    bin_out[...] = bin_ref[...] * (2 * parts)
    distance = lax.broadcasted_iota(jnp.int32, (local_bins, local_bins), 0) - (
        lax.broadcasted_iota(jnp.int32, (local_bins, local_bins), 1)
    )
    window[...] = (jnp.abs(distance) <= HALF_WIN).astype(jnp.float32).astype(jnp.bfloat16)
    write_basis(band * local_bins, local_bins, table)

    source = lax.broadcasted_iota(jnp.int32, (LANES, LANES), 0)
    column = lax.broadcasted_iota(jnp.int32, (LANES, LANES), 1)

    def chosen(inside):
        return inside.astype(jnp.float32).astype(jnp.bfloat16)

    left_weights = [
        chosen((source < HALF_WIN) & (column <= source)),
        chosen((source >= HALF_WIN) & (column <= source - HALF_WIN)),
    ]
    right_weights = [
        chosen((source < HALF_WIN) & (column >= source + HALF_WIN)),
        chosen((source >= HALF_WIN) & (column >= source)),
    ]

    def dot(a, b):
        return jnp.dot(a, b, preferred_element_type=jnp.float32)

    def outside(box, group, weights):
        values = box[group]
        return jnp.concatenate([dot(values, weights[0]), dot(values, weights[1])], axis=0)

    def whiten(group):
        at = pl.ds(pl.multiple_of(group * REACH, REACH), REACH)
        real = near[0, at, :].astype(jnp.float32)
        imag = near[1, at, :].astype(jnp.float32)
        power = real * real + imag * imag
        high = power.astype(jnp.bfloat16)
        low = (power - high.astype(jnp.float32)).astype(jnp.bfloat16)
        total = dot(high, window[...]) + dot(low, window[...])
        for j in range(half):
            columns = slice(j * LANES, (j + 1) * LANES)
            piece = total[:, columns]
            if j == 0:
                piece = piece + outside(left_in, group, left_weights)
            if j == half - 1:
                piece = piece + outside(right_in, group, right_weights)
            scaling = lax.rsqrt(piece / (2 * HALF_WIN + 1) + epsilon)
            for k, part in ((0, real), (1, imag)):
                white = (part[:, columns] * scaling).astype(jnp.bfloat16).astype(jnp.float32)
                rows[pl.ds(group * (REACH * parts) + k * half + j, REACH, stride=parts), :] = white

    for db in (-1, 1):
        arrived(0, db)

    def local(group, carry):
        whiten(group)
        return carry

    lax.fori_loop(1, groups + 1, local, 0)
    for ds, group in ((1, 0), (-1, groups + 1)):
        arrived(ds, 0)
        arrived(ds, -1)
        arrived(ds, 1)

        @pl.when(seg_there[-ds])
        def _():
            whiten(group)
    for ds, db in peers:
        @pl.when(there(ds, db))
        def _():
            sending(ds, db).wait_send()


def pair_kernel(
    local_bins, bins, first_ref, second_ref, bin_ref, rows, table, out_ref, *banks
):
    parts = 2 * local_bins // LANES
    half = parts // 2
    for bank in banks:
        bank[...] = jnp.zeros_like(bank)

    def group(step, carry):
        base = step * BANKS
        updates = []
        for k, bank in enumerate(banks):
            a = pl.multiple_of(first_ref[base + k], parts)
            b = pl.multiple_of(second_ref[base + k], parts)
            o = pl.multiple_of(bin_ref[base + k], 2 * parts)
            first = rows[pl.ds(a, parts), :]
            second = rows[pl.ds(b, parts), :]
            straight = bank[pl.ds(o, parts), :] + first * second
            crossed = bank[pl.ds(o + parts, parts), :] + pltpu.roll(first, half, 0) * second
            updates.append((bank, o, straight, crossed))
        for bank, o, straight, crossed in updates:
            bank[pl.ds(o, parts), :] = straight
            bank[pl.ds(o + parts, parts), :] = crossed
        return carry

    lax.fori_loop(0, first_ref.shape[0] // BANKS, group, 0, unroll=4)

    def stacked(j):
        total = banks[0][pl.ds(j, bins, stride=2 * parts), :]
        for bank in banks[1:]:
            total = total + bank[pl.ds(j, bins, stride=2 * parts), :]
        return total

    lags = jnp.zeros((bins, LAGS), jnp.float32)
    for j in range(parts):
        if j < half:
            piece = stacked(j) + stacked(half + j)
        else:
            piece = stacked(parts + j - half) - stacked(parts + j)
        high = piece.astype(jnp.bfloat16)
        low = (piece - high.astype(jnp.float32)).astype(jnp.bfloat16)
        basis = table[j * LANES : (j + 1) * LANES, :]
        lags += jnp.dot(high, basis, preferred_element_type=jnp.float32)
        lags += jnp.dot(low, basis, preferred_element_type=jnp.float32)
    out_ref[...] = lags


def sum_kernel(segments, bands, lags_ref, out_ref, send, near, mid, far, s1, r1, s2, r2):
    near_count = NEAR_SEGS * bands
    far_count = segments // NEAR_SEGS
    width = LAGS // bands
    seg, band = lax.axis_index("seg"), lax.axis_index("band")
    row, col = seg // NEAR_SEGS, seg % NEAR_SEGS
    me = col * bands + band

    def near_peer(d):
        p = lax.rem(me + d, near_count)
        return p, (row * NEAR_SEGS + p // bands, lax.rem(p, bands))

    def far_peer(d):
        p = lax.rem(row + d, far_count)
        return p, (p * NEAR_SEGS + col, band)

    barrier = pltpu.get_barrier_semaphore()
    for d in range(1, near_count):
        pl.semaphore_signal(barrier, inc=1, device_id=near_peer(d)[1], device_id_type=MESH)
    for d in range(1, far_count):
        pl.semaphore_signal(barrier, inc=1, device_id=far_peer(d)[1], device_id_type=MESH)
    for p in range(near_count):
        c, b = p // bands, p % bands
        block = [
            lags_ref[
                (r * NEAR_SEGS + c) * OB_DEV : (r * NEAR_SEGS + c + 1) * OB_DEV,
                b * width : (b + 1) * width,
            ]
            for r in range(far_count)
        ]
        send[p] = jnp.concatenate(block, axis=0).astype(jnp.bfloat16)
    pl.semaphore_wait(barrier, near_count - 1 + far_count - 1)

    def near_copy(d):
        p, device = near_peer(d)
        return pltpu.make_async_remote_copy(
            src_ref=send.at[p], dst_ref=near.at[d], send_sem=s1.at[d], recv_sem=r1.at[d],
            device_id=device, device_id_type=MESH,
        )

    def far_copy(d):
        p, device = far_peer(d)
        return pltpu.make_async_remote_copy(
            src_ref=mid.at[p], dst_ref=far.at[d], send_sem=s2.at[d], recv_sem=r2.at[d],
            device_id=device, device_id_type=MESH,
        )

    for d in range(1, near_count):
        near_copy(d).start()
    total = send[me].astype(jnp.float32)
    for d in range(1, near_count):
        near_copy(d).wait_recv()
        total += near[d].astype(jnp.float32)
    for r in range(far_count):
        mid[r] = total[r * OB_DEV : (r + 1) * OB_DEV]
    for d in range(1, far_count):
        far_copy(d).start()
    result = mid[row]
    for d in range(1, far_count):
        far_copy(d).wait_recv()
        result += far[d]
    out_ref[...] = result
    for d in range(1, near_count):
        near_copy(d).wait_send()
    for d in range(1, far_count):
        far_copy(d).wait_send()


def whiten(spectra, first, second, bins_at, segments, bands):
    _, channels, local_bins = spectra.shape
    parts = 2 * local_bins // LANES
    groups = channels // REACH
    count = first.shape[0]
    boxed = (count // LANES, LANES)
    vmem = pl.BlockSpec(memory_space=pltpu.VMEM)
    dma = pltpu.SemaphoreType.DMA
    edges = (groups + 2, REACH // 2, LANES)
    index = jax.ShapeDtypeStruct(boxed, jnp.int32)
    rows, table, *indices = pl.pallas_call(
        functools.partial(whiten_kernel, segments, bands),
        out_shape=[
            jax.ShapeDtypeStruct(((channels + 2 * REACH) * parts, LANES), jnp.float32),
            jax.ShapeDtypeStruct((2 * local_bins, LAGS), jnp.bfloat16),
            index, index, index,
        ],
        in_specs=[pl.BlockSpec(memory_space=pl.ANY), vmem, vmem, vmem],
        out_specs=[vmem] * 5,
        scratch_shapes=[
            pltpu.VMEM((2, channels + 2 * REACH, local_bins), jnp.bfloat16),
            pltpu.VMEM((local_bins, local_bins), jnp.bfloat16),
            pltpu.VMEM((2, groups) + edges[1:], jnp.bfloat16),
            pltpu.VMEM(edges, jnp.bfloat16),
            pltpu.VMEM(edges, jnp.bfloat16),
            dma((1,)), dma((8,)), dma((8,)),
        ],
        compiler_params=pltpu.CompilerParams(
            collective_id=0, has_side_effects=True, vmem_limit_bytes=32 * 2**20
        ),
        name="whiten",
    )(spectra, first.reshape(boxed), second.reshape(boxed), bins_at.reshape(boxed))
    return rows, table, [x.reshape(count) for x in indices]


def stack_pairs(rows, table, indices, local_bins, bins):
    parts = 2 * local_bins // LANES
    smem = pl.BlockSpec(memory_space=pltpu.SMEM)
    vmem = pl.BlockSpec(memory_space=pltpu.VMEM)
    return pl.pallas_call(
        functools.partial(pair_kernel, local_bins, bins),
        out_shape=jax.ShapeDtypeStruct((bins, LAGS), jnp.float32),
        in_specs=[smem, smem, smem, vmem, vmem],
        out_specs=vmem,
        scratch_shapes=[pltpu.VMEM((bins * 2 * parts, LANES), jnp.float32)] * BANKS,
        compiler_params=pltpu.CompilerParams(vmem_limit_bytes=32 * 2**20),
        name="pairs",
    )(*indices, rows, table)


def sum_lags(lags, segments, bands):
    near_count, far_count = NEAR_SEGS * bands, segments // NEAR_SEGS
    width = LAGS // bands
    vmem = pl.BlockSpec(memory_space=pltpu.VMEM)
    dma = pltpu.SemaphoreType.DMA
    return pl.pallas_call(
        functools.partial(sum_kernel, segments, bands),
        out_shape=jax.ShapeDtypeStruct((OB_DEV, width), jnp.float32),
        in_specs=[vmem],
        out_specs=vmem,
        scratch_shapes=[
            pltpu.VMEM((near_count, far_count * OB_DEV, width), jnp.bfloat16),
            pltpu.VMEM((near_count, far_count * OB_DEV, width), jnp.bfloat16),
            pltpu.VMEM((far_count, OB_DEV, width), jnp.float32),
            pltpu.VMEM((far_count, OB_DEV, width), jnp.float32),
            dma((near_count,)), dma((near_count,)), dma((far_count,)), dma((far_count,)),
        ],
        compiler_params=pltpu.CompilerParams(
            collective_id=1, has_side_effects=True, vmem_limit_bytes=32 * 2**20
        ),
        name="sums",
    )(lags)


def per_device(spectra, pair_first, pair_second, pair_bin):
    segments, bands = lax.axis_size("seg"), lax.axis_size("band")
    rows, table, indices = whiten(spectra, pair_first, pair_second, pair_bin, segments, bands)
    lags = stack_pairs(rows, table, indices, spectra.shape[2], segments * OB_DEV)
    return sum_lags(lags, segments, bands)


def solution(mesh):
    placed = (P(None, "seg", "band"), P("seg"), P("seg"), P("seg"))
    return jax.shard_map(
        per_device, mesh=mesh, in_specs=placed, out_specs=P("seg", "band"), check_vma=False
    )
```

```python
import functools
import math

import jax
import jax.numpy as jnp
from jax import lax
from jax.experimental import pallas as pl
from jax.experimental.pallas import tpu as pltpu
from jax.sharding import PartitionSpec as P

OB_DEV = 8
REACH = 256
FREQ = 1024
LAGS = 1024
HALF_WIN = 64
BANKS = 8
LANES = 128
FINE = 32
NEAR_SEGS = 4
MESH = pl.DeviceIdType.MESH

epsilon = 1e-06


def circle(first, step, count):
    rows = lax.broadcasted_iota(jnp.int32, (count, LAGS), 0) * step + first
    lags = lax.broadcasted_iota(jnp.int32, (count, LAGS), 1) - LAGS // 2
    residue = jnp.bitwise_and(rows * lags, 2 * FREQ - 1)
    residue = residue - jnp.where(residue >= FREQ, 2 * FREQ, 0)
    angles = residue.astype(jnp.float32) * (math.pi / FREQ)
    return jnp.cos(angles), jnp.sin(angles)


def write_basis(first_bin, local_bins, table):
    coarse_cos, coarse_sin = circle(first_bin, FINE, local_bins // FINE)
    fine_cos, fine_sin = circle(0, 1, FINE)
    fine_cos, fine_sin = fine_cos * (1.0 / FREQ), fine_sin * (1.0 / FREQ)
    for i in range(local_bins // FINE):
        cc, cs = coarse_cos[i : i + 1], coarse_sin[i : i + 1]
        table[i * FINE : (i + 1) * FINE, :] = (cc * fine_cos - cs * fine_sin).astype(jnp.bfloat16)
        table[local_bins + i * FINE : local_bins + (i + 1) * FINE, :] = (
            -(cs * fine_cos + cc * fine_sin)
        ).astype(jnp.bfloat16)


def whiten_kernel(
    segments, bands, spectra_ref, first_ref, second_ref, bin_ref,
    rows, table, first_out, second_out, bin_out,
    near, window, edge_out, left_in, right_in, index_in, load_sem, send_sem, recv_sem,
):
    channels, local_bins = spectra_ref.shape[1:]
    groups = channels // REACH
    parts = 2 * local_bins // LANES
    half = parts // 2
    packed = REACH // 2
    seg, band = lax.axis_index("seg"), lax.axis_index("band")

    seg_there = {-1: seg > 0, 0: None, 1: seg < segments - 1}
    band_there = {-1: band > 0, 0: None, 1: band < bands - 1}
    peers = [(ds, db) for ds in (-1, 0, 1) for db in (-1, 0, 1) if (ds, db) != (0, 0)]

    def there(ds, db):
        if ds == 0:
            return band_there[db]
        if db == 0:
            return seg_there[ds]
        return jnp.logical_and(seg_there[ds], band_there[db])

    load = pltpu.make_async_copy(
        spectra_ref, near.at[:, pl.ds(REACH, channels), :], load_sem.at[0]
    )
    load.start()
    index_loads = [
        pltpu.make_async_copy(ref, index_in.at[k], load_sem.at[1 + k])
        for k, ref in enumerate((first_ref, second_ref, bin_ref))
    ]
    for index_load in index_loads:
        index_load.start()
    barrier = pltpu.get_barrier_semaphore()
    for ds, db in peers:
        @pl.when(there(ds, db))
        def _():
            pl.semaphore_signal(
                barrier, inc=1, device_id=(seg + ds, band + db), device_id_type=MESH
            )
    seg_span = 3 - jnp.where(seg == 0, 1, 0) - jnp.where(seg == segments - 1, 1, 0)
    band_span = 3 - jnp.where(band == 0, 1, 0) - jnp.where(band == bands - 1, 1, 0)
    pl.semaphore_wait(barrier, seg_span * band_span - 1)

    def sending(ds, db):
        slot = peers.index((ds, db))
        if db == 0:
            source = spectra_ref.at[:, pl.ds(channels - REACH if ds > 0 else 0, REACH), :]
            target = near.at[:, pl.ds(0 if ds > 0 else REACH + channels, REACH), :]
        else:
            side, box = (1, left_in) if db > 0 else (0, right_in)
            if ds == 0:
                source = edge_out.at[side]
                target = box.at[pl.ds(1, groups)]
            else:
                source = edge_out.at[side, pl.ds(groups - 1 if ds > 0 else 0, 1)]
                target = box.at[pl.ds(0 if ds > 0 else groups + 1, 1)]
        return pltpu.make_async_remote_copy(
            src_ref=source, dst_ref=target, send_sem=send_sem.at[slot],
            recv_sem=recv_sem.at[slot], device_id=(seg + ds, band + db), device_id_type=MESH,
        )

    def start(ds, db):
        @pl.when(there(ds, db))
        def _():
            sending(ds, db).start()

    def arrived(ds, db):
        @pl.when(there(-ds, -db))
        def _():
            sending(ds, db).wait_recv()

    start(-1, 0)
    start(1, 0)
    load.wait()

    lane = lax.broadcasted_iota(jnp.int32, (packed, LANES), 1)

    def edge(side, group):
        at = 0 if side == 0 else local_bins - LANES
        real = near[0, pl.ds(REACH + group * REACH, REACH), at : at + LANES].astype(jnp.float32)
        imag = near[1, pl.ds(REACH + group * REACH, REACH), at : at + LANES].astype(jnp.float32)
        power = real * real + imag * imag
        upper, lower = power[:packed], power[packed:]
        if side == 0:
            both = jnp.where(lane < HALF_WIN, upper, pltpu.roll(lower, HALF_WIN, 1))
        else:
            both = jnp.where(lane < HALF_WIN, pltpu.roll(upper, HALF_WIN, 1), lower)
        edge_out[side, group] = both.astype(jnp.bfloat16)

    for side, db in ((0, -1), (1, 1)):
        @pl.when(band_there[db])
        def _():
            for group in range(groups):
                edge(side, group)
        start(0, db)
        start(-1, db)
        start(1, db)
    for db, box in ((-1, left_in), (1, right_in)):
        @pl.when(jnp.logical_not(band_there[db]))
        def _():
            box[...] = jnp.zeros_like(box)

    shift = REACH - seg * channels
    for index_load in index_loads:
        index_load.wait()
    first_out[...] = (index_in[0] + shift) * parts
    second_out[...] = (index_in[1] + shift) * parts
    bin_out[...] = index_in[2] * parts
    distance = lax.broadcasted_iota(jnp.int32, (local_bins, local_bins), 0) - (
        lax.broadcasted_iota(jnp.int32, (local_bins, local_bins), 1)
    )
    window[...] = (jnp.abs(distance) <= HALF_WIN).astype(jnp.float32).astype(jnp.bfloat16)
    write_basis(band * local_bins, local_bins, table)

    source = lax.broadcasted_iota(jnp.int32, (LANES, LANES), 0)
    column = lax.broadcasted_iota(jnp.int32, (LANES, LANES), 1)

    def chosen(inside):
        return inside.astype(jnp.float32).astype(jnp.bfloat16)

    left_weights = [
        chosen((source < HALF_WIN) & (column <= source)),
        chosen((source >= HALF_WIN) & (column <= source - HALF_WIN)),
    ]
    right_weights = [
        chosen((source < HALF_WIN) & (column >= source + HALF_WIN)),
        chosen((source >= HALF_WIN) & (column >= source)),
    ]

    def dot(a, b):
        return jnp.dot(a, b, preferred_element_type=jnp.float32)

    def outside(box, group, weights):
        values = box[group]
        return jnp.concatenate([dot(values, weights[0]), dot(values, weights[1])], axis=0)

    def whiten(group):
        at = pl.ds(pl.multiple_of(group * REACH, REACH), REACH)
        real = near[0, at, :].astype(jnp.float32)
        imag = near[1, at, :].astype(jnp.float32)
        power = real * real + imag * imag
        high = power.astype(jnp.bfloat16)
        low = (power - high.astype(jnp.float32)).astype(jnp.bfloat16)
        total = dot(high, window[...]) + dot(low, window[...])
        for j in range(half):
            columns = slice(j * LANES, (j + 1) * LANES)
            piece = total[:, columns]
            if j == 0:
                piece = piece + outside(left_in, group, left_weights)
            if j == half - 1:
                piece = piece + outside(right_in, group, right_weights)
            scaling = lax.rsqrt(piece / (2 * HALF_WIN + 1) + epsilon)
            for k, part in ((0, real), (1, imag)):
                white = (part[:, columns] * scaling).astype(jnp.bfloat16).astype(jnp.float32)
                rows[pl.ds(group * (REACH * parts) + k * half + j, REACH, stride=parts), :] = white

    for db in (-1, 1):
        arrived(0, db)

    def local(group, carry):
        whiten(group)
        return carry

    lax.fori_loop(1, groups + 1, local, 0)
    for ds, group in ((1, 0), (-1, groups + 1)):
        arrived(ds, 0)
        arrived(ds, -1)
        arrived(ds, 1)

        @pl.when(seg_there[-ds])
        def _():
            whiten(group)
    for ds, db in peers:
        @pl.when(there(ds, db))
        def _():
            sending(ds, db).wait_send()


def pair_kernel(
    local_bins, bins, first_ref, second_ref, bin_ref, rows, table, out_ref, *banks
):
    parts = 2 * local_bins // LANES
    half = parts // 2
    for bank in banks:
        bank[...] = jnp.zeros_like(bank)

    upper = lax.broadcasted_iota(jnp.int32, (parts, LANES), 0) < half

    def group(step, carry):
        base = step * BANKS
        updates = []
        for k, bank in enumerate(banks):
            a = pl.multiple_of(first_ref[base + k], parts)
            b = pl.multiple_of(second_ref[base + k], parts)
            o = pl.multiple_of(bin_ref[base + k], parts)
            first = rows[pl.ds(a, parts), :]
            second = rows[pl.ds(b, parts), :]
            turned = pltpu.roll(second, half, 0)
            real = jnp.where(upper, second, turned)
            imag = jnp.where(upper, turned, -second)
            cross = first * real + pltpu.roll(first, half, 0) * imag
            updates.append((bank, o, bank[pl.ds(o, parts), :] + cross))
        for bank, o, updated in updates:
            bank[pl.ds(o, parts), :] = updated
        return carry

    lax.fori_loop(0, first_ref.shape[0] // BANKS, group, 0, unroll=2)

    lags = jnp.zeros((bins, LAGS), jnp.float32)
    for j in range(parts):
        piece = banks[0][pl.ds(j, bins, stride=parts), :]
        for bank in banks[1:]:
            piece = piece + bank[pl.ds(j, bins, stride=parts), :]
        high = piece.astype(jnp.bfloat16)
        low = (piece - high.astype(jnp.float32)).astype(jnp.bfloat16)
        basis = table[j * LANES : (j + 1) * LANES, :]
        lags += jnp.dot(high, basis, preferred_element_type=jnp.float32)
        lags += jnp.dot(low, basis, preferred_element_type=jnp.float32)
    out_ref[...] = lags


def sum_kernel(segments, bands, lags_ref, out_ref, send, near, mid, far, s1, r1, s2, r2):
    near_count = NEAR_SEGS * bands
    far_count = segments // NEAR_SEGS
    width = LAGS // bands
    seg, band = lax.axis_index("seg"), lax.axis_index("band")
    row, col = seg // NEAR_SEGS, seg % NEAR_SEGS
    me = col * bands + band

    def near_peer(d):
        p = lax.rem(me + d, near_count)
        return p, (row * NEAR_SEGS + p // bands, lax.rem(p, bands))

    def far_peer(d):
        p = lax.rem(row + d, far_count)
        return p, (p * NEAR_SEGS + col, band)

    barrier = pltpu.get_barrier_semaphore()
    for d in range(1, near_count):
        pl.semaphore_signal(barrier, inc=1, device_id=near_peer(d)[1], device_id_type=MESH)
    for d in range(1, far_count):
        pl.semaphore_signal(barrier, inc=1, device_id=far_peer(d)[1], device_id_type=MESH)
    for p in range(near_count):
        c, b = p // bands, p % bands
        block = [
            lags_ref[
                (r * NEAR_SEGS + c) * OB_DEV : (r * NEAR_SEGS + c + 1) * OB_DEV,
                b * width : (b + 1) * width,
            ]
            for r in range(far_count)
        ]
        send[p] = jnp.concatenate(block, axis=0).astype(jnp.bfloat16)
    pl.semaphore_wait(barrier, near_count - 1 + far_count - 1)

    def near_copy(d):
        p, device = near_peer(d)
        return pltpu.make_async_remote_copy(
            src_ref=send.at[p], dst_ref=near.at[d], send_sem=s1.at[d], recv_sem=r1.at[d],
            device_id=device, device_id_type=MESH,
        )

    def far_copy(d):
        p, device = far_peer(d)
        return pltpu.make_async_remote_copy(
            src_ref=mid.at[p], dst_ref=far.at[d], send_sem=s2.at[d], recv_sem=r2.at[d],
            device_id=device, device_id_type=MESH,
        )

    for d in range(1, near_count):
        near_copy(d).start()
    total = send[me].astype(jnp.float32)
    for d in range(1, near_count):
        near_copy(d).wait_recv()
        total += near[d].astype(jnp.float32)
    for r in range(far_count):
        mid[r] = total[r * OB_DEV : (r + 1) * OB_DEV]
    for d in range(1, far_count):
        far_copy(d).start()
    result = mid[row]
    for d in range(1, far_count):
        far_copy(d).wait_recv()
        result += far[d]
    out_ref[...] = result
    for d in range(1, near_count):
        near_copy(d).wait_send()
    for d in range(1, far_count):
        far_copy(d).wait_send()


def whiten(spectra, first, second, bins_at, segments, bands):
    _, channels, local_bins = spectra.shape
    parts = 2 * local_bins // LANES
    groups = channels // REACH
    count = first.shape[0]
    boxed = (count // LANES, LANES)
    vmem = pl.BlockSpec(memory_space=pltpu.VMEM)
    dma = pltpu.SemaphoreType.DMA
    edges = (groups + 2, REACH // 2, LANES)
    index = jax.ShapeDtypeStruct(boxed, jnp.int32)
    rows, table, *indices = pl.pallas_call(
        functools.partial(whiten_kernel, segments, bands),
        out_shape=[
            jax.ShapeDtypeStruct(((channels + 2 * REACH) * parts, LANES), jnp.float32),
            jax.ShapeDtypeStruct((2 * local_bins, LAGS), jnp.bfloat16),
            index, index, index,
        ],
        in_specs=[pl.BlockSpec(memory_space=pltpu.HBM)] * 4,
        out_specs=[vmem] * 5,
        scratch_shapes=[
            pltpu.VMEM((2, channels + 2 * REACH, local_bins), jnp.bfloat16),
            pltpu.VMEM((local_bins, local_bins), jnp.bfloat16),
            pltpu.VMEM((2, groups) + edges[1:], jnp.bfloat16),
            pltpu.VMEM(edges, jnp.bfloat16),
            pltpu.VMEM(edges, jnp.bfloat16),
            pltpu.VMEM((3,) + boxed, jnp.int32),
            dma((4,)), dma((8,)), dma((8,)),
        ],
        compiler_params=pltpu.CompilerParams(
            collective_id=0, has_side_effects=True, vmem_limit_bytes=32 * 2**20
        ),
        name="whiten",
    )(spectra, first.reshape(boxed), second.reshape(boxed), bins_at.reshape(boxed))
    return rows, table, [x.reshape(count) for x in indices]


def stack_pairs(rows, table, indices, local_bins, bins):
    parts = 2 * local_bins // LANES
    smem = pl.BlockSpec(memory_space=pltpu.SMEM)
    vmem = pl.BlockSpec(memory_space=pltpu.VMEM)
    return pl.pallas_call(
        functools.partial(pair_kernel, local_bins, bins),
        out_shape=jax.ShapeDtypeStruct((bins, LAGS), jnp.float32),
        in_specs=[smem, smem, smem, vmem, vmem],
        out_specs=vmem,
        scratch_shapes=[pltpu.VMEM((bins * parts, LANES), jnp.float32)] * BANKS,
        compiler_params=pltpu.CompilerParams(vmem_limit_bytes=32 * 2**20),
        name="pairs",
    )(*indices, rows, table)


def sum_lags(lags, segments, bands):
    near_count, far_count = NEAR_SEGS * bands, segments // NEAR_SEGS
    width = LAGS // bands
    vmem = pl.BlockSpec(memory_space=pltpu.VMEM)
    dma = pltpu.SemaphoreType.DMA
    return pl.pallas_call(
        functools.partial(sum_kernel, segments, bands),
        out_shape=jax.ShapeDtypeStruct((OB_DEV, width), jnp.float32),
        in_specs=[vmem],
        out_specs=vmem,
        scratch_shapes=[
            pltpu.VMEM((near_count, far_count * OB_DEV, width), jnp.bfloat16),
            pltpu.VMEM((near_count, far_count * OB_DEV, width), jnp.bfloat16),
            pltpu.VMEM((far_count, OB_DEV, width), jnp.float32),
            pltpu.VMEM((far_count, OB_DEV, width), jnp.float32),
            dma((near_count,)), dma((near_count,)), dma((far_count,)), dma((far_count,)),
        ],
        compiler_params=pltpu.CompilerParams(
            collective_id=1, has_side_effects=True, vmem_limit_bytes=32 * 2**20
        ),
        name="sums",
    )(lags)


def per_device(spectra, pair_first, pair_second, pair_bin):
    segments, bands = lax.axis_size("seg"), lax.axis_size("band")
    rows, table, indices = whiten(spectra, pair_first, pair_second, pair_bin, segments, bands)
    lags = stack_pairs(rows, table, indices, spectra.shape[2], segments * OB_DEV)
    return sum_lags(lags, segments, bands)


def solution(mesh):
    placed = (P(None, "seg", "band"), P("seg"), P("seg"), P("seg"))
    return jax.shard_map(
        per_device, mesh=mesh, in_specs=placed, out_specs=P("seg", "band"), check_vma=False
    )
```

```python
import functools
import math

import jax
import jax.numpy as jnp
from jax import lax
from jax.experimental import pallas as pl
from jax.experimental.pallas import tpu as pltpu
from jax.sharding import PartitionSpec as P

OB_DEV = 8
REACH = 256
FREQ = 1024
LAGS = 1024
HALF_WIN = 64
BANKS = 8
LANES = 128
FINE = 32
NEAR_SEGS = 4
MESH = pl.DeviceIdType.MESH

epsilon = 1e-06


def circle(first, step, count):
    rows = lax.broadcasted_iota(jnp.int32, (count, LAGS), 0) * step + first
    lags = lax.broadcasted_iota(jnp.int32, (count, LAGS), 1) - LAGS // 2
    residue = jnp.bitwise_and(rows * lags, 2 * FREQ - 1)
    residue = residue - jnp.where(residue >= FREQ, 2 * FREQ, 0)
    angles = residue.astype(jnp.float32) * (math.pi / FREQ)
    return jnp.cos(angles), jnp.sin(angles)


def write_basis(first_bin, local_bins, table):
    coarse_cos, coarse_sin = circle(first_bin, FINE, local_bins // FINE)
    fine_cos, fine_sin = circle(0, 1, FINE)
    fine_cos, fine_sin = fine_cos * (1.0 / FREQ), fine_sin * (1.0 / FREQ)
    for i in range(local_bins // FINE):
        cc, cs = coarse_cos[i : i + 1], coarse_sin[i : i + 1]
        table[i * FINE : (i + 1) * FINE, :] = (cc * fine_cos - cs * fine_sin).astype(jnp.bfloat16)
        table[local_bins + i * FINE : local_bins + (i + 1) * FINE, :] = (
            -(cs * fine_cos + cc * fine_sin)
        ).astype(jnp.bfloat16)


def whiten_kernel(
    segments, bands, spectra_ref, first_ref, second_ref, bin_ref,
    rows, table, first_out, second_out, bin_out,
    near, window, edge_out, left_in, right_in, index_in, load_sem, send_sem, recv_sem,
):
    channels, local_bins = spectra_ref.shape[1:]
    groups = channels // REACH
    parts = 2 * local_bins // LANES
    half = parts // 2
    packed = REACH // 2
    seg, band = lax.axis_index("seg"), lax.axis_index("band")

    seg_there = {-1: seg > 0, 0: None, 1: seg < segments - 1}
    band_there = {-1: band > 0, 0: None, 1: band < bands - 1}
    peers = [(ds, db) for ds in (-1, 0, 1) for db in (-1, 0, 1) if (ds, db) != (0, 0)]

    def there(ds, db):
        if ds == 0:
            return band_there[db]
        if db == 0:
            return seg_there[ds]
        return jnp.logical_and(seg_there[ds], band_there[db])

    load = pltpu.make_async_copy(
        spectra_ref, near.at[:, pl.ds(REACH, channels), :], load_sem.at[0]
    )
    load.start()
    index_loads = [
        pltpu.make_async_copy(ref, index_in.at[k], load_sem.at[1 + k])
        for k, ref in enumerate((first_ref, second_ref, bin_ref))
    ]
    for index_load in index_loads:
        index_load.start()
    barrier = pltpu.get_barrier_semaphore()
    for ds, db in peers:
        @pl.when(there(ds, db))
        def _():
            pl.semaphore_signal(
                barrier, inc=1, device_id=(seg + ds, band + db), device_id_type=MESH
            )
    seg_span = 3 - jnp.where(seg == 0, 1, 0) - jnp.where(seg == segments - 1, 1, 0)
    band_span = 3 - jnp.where(band == 0, 1, 0) - jnp.where(band == bands - 1, 1, 0)
    pl.semaphore_wait(barrier, seg_span * band_span - 1)

    def sending(ds, db):
        slot = peers.index((ds, db))
        if db == 0:
            source = spectra_ref.at[:, pl.ds(channels - REACH if ds > 0 else 0, REACH), :]
            target = near.at[:, pl.ds(0 if ds > 0 else REACH + channels, REACH), :]
        else:
            side, box = (1, left_in) if db > 0 else (0, right_in)
            if ds == 0:
                source = edge_out.at[side]
                target = box.at[pl.ds(1, groups)]
            else:
                source = edge_out.at[side, pl.ds(groups - 1 if ds > 0 else 0, 1)]
                target = box.at[pl.ds(0 if ds > 0 else groups + 1, 1)]
        return pltpu.make_async_remote_copy(
            src_ref=source, dst_ref=target, send_sem=send_sem.at[slot],
            recv_sem=recv_sem.at[slot], device_id=(seg + ds, band + db), device_id_type=MESH,
        )

    def start(ds, db):
        @pl.when(there(ds, db))
        def _():
            sending(ds, db).start()

    def arrived(ds, db):
        @pl.when(there(-ds, -db))
        def _():
            sending(ds, db).wait_recv()

    start(-1, 0)
    start(1, 0)
    load.wait()

    lane = lax.broadcasted_iota(jnp.int32, (packed, LANES), 1)

    def edge(side, group):
        at = 0 if side == 0 else local_bins - LANES
        real = near[0, pl.ds(REACH + group * REACH, REACH), at : at + LANES].astype(jnp.float32)
        imag = near[1, pl.ds(REACH + group * REACH, REACH), at : at + LANES].astype(jnp.float32)
        power = real * real + imag * imag
        upper, lower = power[:packed], power[packed:]
        if side == 0:
            both = jnp.where(lane < HALF_WIN, upper, pltpu.roll(lower, HALF_WIN, 1))
        else:
            both = jnp.where(lane < HALF_WIN, pltpu.roll(upper, HALF_WIN, 1), lower)
        edge_out[side, group] = both.astype(jnp.bfloat16)

    for side, db in ((0, -1), (1, 1)):
        @pl.when(band_there[db])
        def _():
            for group in range(groups):
                edge(side, group)
        start(0, db)
        start(-1, db)
        start(1, db)
    for db, box in ((-1, left_in), (1, right_in)):
        @pl.when(jnp.logical_not(band_there[db]))
        def _():
            box[...] = jnp.zeros_like(box)

    shift = REACH - seg * channels
    for index_load in index_loads:
        index_load.wait()
    first_out[...] = index_in[0] + shift
    second_out[...] = index_in[1] + shift
    bin_out[...] = index_in[2]
    distance = lax.broadcasted_iota(jnp.int32, (local_bins, local_bins), 0) - (
        lax.broadcasted_iota(jnp.int32, (local_bins, local_bins), 1)
    )
    window[...] = (jnp.abs(distance) <= HALF_WIN).astype(jnp.float32).astype(jnp.bfloat16)
    write_basis(band * local_bins, local_bins, table)

    source = lax.broadcasted_iota(jnp.int32, (LANES, LANES), 0)
    column = lax.broadcasted_iota(jnp.int32, (LANES, LANES), 1)

    def chosen(inside):
        return inside.astype(jnp.float32).astype(jnp.bfloat16)

    left_weights = [
        chosen((source < HALF_WIN) & (column <= source)),
        chosen((source >= HALF_WIN) & (column <= source - HALF_WIN)),
    ]
    right_weights = [
        chosen((source < HALF_WIN) & (column >= source + HALF_WIN)),
        chosen((source >= HALF_WIN) & (column >= source)),
    ]

    def dot(a, b):
        return jnp.dot(a, b, preferred_element_type=jnp.float32)

    def outside(box, group, weights):
        values = box[group]
        return jnp.concatenate([dot(values, weights[0]), dot(values, weights[1])], axis=0)

    def whiten(group):
        at = pl.ds(pl.multiple_of(group * REACH, REACH), REACH)
        real = near[0, at, :].astype(jnp.float32)
        imag = near[1, at, :].astype(jnp.float32)
        power = real * real + imag * imag
        high = power.astype(jnp.bfloat16)
        low = (power - high.astype(jnp.float32)).astype(jnp.bfloat16)
        total = dot(high, window[...]) + dot(low, window[...])
        for j in range(half):
            columns = slice(j * LANES, (j + 1) * LANES)
            piece = total[:, columns]
            if j == 0:
                piece = piece + outside(left_in, group, left_weights)
            if j == half - 1:
                piece = piece + outside(right_in, group, right_weights)
            scaling = lax.rsqrt(piece / (2 * HALF_WIN + 1) + epsilon)
            for k, part in ((0, real), (1, imag)):
                white = (part[:, columns] * scaling).astype(jnp.bfloat16).astype(jnp.float32)
                rows[pl.ds(group * (REACH * parts) + k * half + j, REACH, stride=parts), :] = white

    for db in (-1, 1):
        arrived(0, db)

    def local(group, carry):
        whiten(group)
        return carry

    lax.fori_loop(1, groups + 1, local, 0)
    for ds, group in ((1, 0), (-1, groups + 1)):
        arrived(ds, 0)
        arrived(ds, -1)
        arrived(ds, 1)

        @pl.when(seg_there[-ds])
        def _():
            whiten(group)
    for ds, db in peers:
        @pl.when(there(ds, db))
        def _():
            sending(ds, db).wait_send()


def pair_kernel(
    local_bins, bins, first_ref, second_ref, bin_ref, rows, table, out_ref, *banks
):
    parts = 2 * local_bins // LANES
    half = parts // 2
    for bank in banks:
        bank[...] = jnp.zeros_like(bank)

    upper = lax.broadcasted_iota(jnp.int32, (parts, LANES), 0) < half

    def group(step, carry):
        base = step * BANKS
        updates = []
        for k, bank in enumerate(banks):
            o = bin_ref[base + k]
            first = rows[first_ref[base + k]]
            second = rows[second_ref[base + k]]
            turned = pltpu.roll(second, half, 0)
            real = jnp.where(upper, second, turned)
            imag = jnp.where(upper, turned, -second)
            cross = first * real + pltpu.roll(first, half, 0) * imag
            updates.append((bank, o, bank[o] + cross))
        for bank, o, updated in updates:
            bank[o] = updated
        return carry

    lax.fori_loop(0, first_ref.shape[0] // BANKS, group, 0, unroll=2)

    lags = jnp.zeros((bins, LAGS), jnp.float32)
    for j in range(parts):
        piece = banks[0][:, j, :]
        for bank in banks[1:]:
            piece = piece + bank[:, j, :]
        high = piece.astype(jnp.bfloat16)
        low = (piece - high.astype(jnp.float32)).astype(jnp.bfloat16)
        basis = table[j * LANES : (j + 1) * LANES, :]
        lags += jnp.dot(high, basis, preferred_element_type=jnp.float32)
        lags += jnp.dot(low, basis, preferred_element_type=jnp.float32)
    out_ref[...] = lags


def sum_kernel(segments, bands, lags_ref, out_ref, send, near, mid, far, s1, r1, s2, r2):
    near_count = NEAR_SEGS * bands
    far_count = segments // NEAR_SEGS
    width = LAGS // bands
    seg, band = lax.axis_index("seg"), lax.axis_index("band")
    row, col = seg // NEAR_SEGS, seg % NEAR_SEGS
    me = col * bands + band

    def near_peer(d):
        p = lax.rem(me + d, near_count)
        return p, (row * NEAR_SEGS + p // bands, lax.rem(p, bands))

    def far_peer(d):
        p = lax.rem(row + d, far_count)
        return p, (p * NEAR_SEGS + col, band)

    barrier = pltpu.get_barrier_semaphore()
    for d in range(1, near_count):
        pl.semaphore_signal(barrier, inc=1, device_id=near_peer(d)[1], device_id_type=MESH)
    for d in range(1, far_count):
        pl.semaphore_signal(barrier, inc=1, device_id=far_peer(d)[1], device_id_type=MESH)
    for p in range(near_count):
        c, b = p // bands, p % bands
        block = [
            lags_ref[
                (r * NEAR_SEGS + c) * OB_DEV : (r * NEAR_SEGS + c + 1) * OB_DEV,
                b * width : (b + 1) * width,
            ]
            for r in range(far_count)
        ]
        send[p] = jnp.concatenate(block, axis=0).astype(jnp.bfloat16)
    pl.semaphore_wait(barrier, near_count - 1 + far_count - 1)

    def near_copy(d):
        p, device = near_peer(d)
        return pltpu.make_async_remote_copy(
            src_ref=send.at[p], dst_ref=near.at[d], send_sem=s1.at[d], recv_sem=r1.at[d],
            device_id=device, device_id_type=MESH,
        )

    def far_copy(d):
        p, device = far_peer(d)
        return pltpu.make_async_remote_copy(
            src_ref=mid.at[p], dst_ref=far.at[d], send_sem=s2.at[d], recv_sem=r2.at[d],
            device_id=device, device_id_type=MESH,
        )

    for d in range(1, near_count):
        near_copy(d).start()
    total = send[me].astype(jnp.float32)
    for d in range(1, near_count):
        near_copy(d).wait_recv()
        total += near[d].astype(jnp.float32)
    for r in range(far_count):
        mid[r] = total[r * OB_DEV : (r + 1) * OB_DEV]
    for d in range(1, far_count):
        far_copy(d).start()
    result = mid[row]
    for d in range(1, far_count):
        far_copy(d).wait_recv()
        result += far[d]
    out_ref[...] = result
    for d in range(1, near_count):
        near_copy(d).wait_send()
    for d in range(1, far_count):
        far_copy(d).wait_send()


def whiten(spectra, first, second, bins_at, segments, bands):
    _, channels, local_bins = spectra.shape
    parts = 2 * local_bins // LANES
    groups = channels // REACH
    count = first.shape[0]
    boxed = (count // LANES, LANES)
    vmem = pl.BlockSpec(memory_space=pltpu.VMEM)
    dma = pltpu.SemaphoreType.DMA
    edges = (groups + 2, REACH // 2, LANES)
    index = jax.ShapeDtypeStruct(boxed, jnp.int32)
    rows, table, *indices = pl.pallas_call(
        functools.partial(whiten_kernel, segments, bands),
        out_shape=[
            jax.ShapeDtypeStruct(((channels + 2 * REACH) * parts, LANES), jnp.float32),
            jax.ShapeDtypeStruct((2 * local_bins, LAGS), jnp.bfloat16),
            index, index, index,
        ],
        in_specs=[pl.BlockSpec(memory_space=pltpu.HBM)] * 4,
        out_specs=[vmem] * 5,
        scratch_shapes=[
            pltpu.VMEM((2, channels + 2 * REACH, local_bins), jnp.bfloat16),
            pltpu.VMEM((local_bins, local_bins), jnp.bfloat16),
            pltpu.VMEM((2, groups) + edges[1:], jnp.bfloat16),
            pltpu.VMEM(edges, jnp.bfloat16),
            pltpu.VMEM(edges, jnp.bfloat16),
            pltpu.VMEM((3,) + boxed, jnp.int32),
            dma((4,)), dma((8,)), dma((8,)),
        ],
        compiler_params=pltpu.CompilerParams(
            collective_id=0, has_side_effects=True, vmem_limit_bytes=32 * 2**20
        ),
        name="whiten",
    )(spectra, first.reshape(boxed), second.reshape(boxed), bins_at.reshape(boxed))
    return rows, table, [x.reshape(count) for x in indices]


def stack_pairs(rows, table, indices, local_bins, bins):
    parts = 2 * local_bins // LANES
    smem = pl.BlockSpec(memory_space=pltpu.SMEM)
    vmem = pl.BlockSpec(memory_space=pltpu.VMEM)
    return pl.pallas_call(
        functools.partial(pair_kernel, local_bins, bins),
        out_shape=jax.ShapeDtypeStruct((bins, LAGS), jnp.float32),
        in_specs=[smem, smem, smem, vmem, vmem],
        out_specs=vmem,
        scratch_shapes=[pltpu.VMEM((bins, parts, LANES), jnp.float32)] * BANKS,
        compiler_params=pltpu.CompilerParams(vmem_limit_bytes=32 * 2**20),
        name="pairs",
    )(*indices, rows.reshape(-1, parts, LANES), table)


def sum_lags(lags, segments, bands):
    near_count, far_count = NEAR_SEGS * bands, segments // NEAR_SEGS
    width = LAGS // bands
    vmem = pl.BlockSpec(memory_space=pltpu.VMEM)
    dma = pltpu.SemaphoreType.DMA
    return pl.pallas_call(
        functools.partial(sum_kernel, segments, bands),
        out_shape=jax.ShapeDtypeStruct((OB_DEV, width), jnp.float32),
        in_specs=[vmem],
        out_specs=vmem,
        scratch_shapes=[
            pltpu.VMEM((near_count, far_count * OB_DEV, width), jnp.bfloat16),
            pltpu.VMEM((near_count, far_count * OB_DEV, width), jnp.bfloat16),
            pltpu.VMEM((far_count, OB_DEV, width), jnp.float32),
            pltpu.VMEM((far_count, OB_DEV, width), jnp.float32),
            dma((near_count,)), dma((near_count,)), dma((far_count,)), dma((far_count,)),
        ],
        compiler_params=pltpu.CompilerParams(
            collective_id=1, has_side_effects=True, vmem_limit_bytes=32 * 2**20
        ),
        name="sums",
    )(lags)


def per_device(spectra, pair_first, pair_second, pair_bin):
    segments, bands = lax.axis_size("seg"), lax.axis_size("band")
    rows, table, indices = whiten(spectra, pair_first, pair_second, pair_bin, segments, bands)
    lags = stack_pairs(rows, table, indices, spectra.shape[2], segments * OB_DEV)
    return sum_lags(lags, segments, bands)


def solution(mesh):
    placed = (P(None, "seg", "band"), P("seg"), P("seg"), P("seg"))
    return jax.shard_map(
        per_device, mesh=mesh, in_specs=placed, out_specs=P("seg", "band"), check_vma=False
    )
```

```python
import functools
import math

import jax
import jax.numpy as jnp
from jax import lax
from jax.experimental import pallas as pl
from jax.experimental.pallas import tpu as pltpu
from jax.sharding import PartitionSpec as P

OB_DEV = 8
REACH = 256
FREQ = 1024
LAGS = 1024
HALF_WIN = 64
BANKS = 4
LANES = 128
FINE = 32
NEAR_SEGS = 4
MESH = pl.DeviceIdType.MESH

epsilon = 1e-06


def circle(first, step, count):
    rows = lax.broadcasted_iota(jnp.int32, (count, LAGS), 0) * step + first
    lags = lax.broadcasted_iota(jnp.int32, (count, LAGS), 1) - LAGS // 2
    residue = jnp.bitwise_and(rows * lags, 2 * FREQ - 1)
    residue = residue - jnp.where(residue >= FREQ, 2 * FREQ, 0)
    angles = residue.astype(jnp.float32) * (math.pi / FREQ)
    return jnp.cos(angles), jnp.sin(angles)


def write_basis(first_bin, local_bins, table):
    coarse_cos, coarse_sin = circle(first_bin, FINE, local_bins // FINE)
    fine_cos, fine_sin = circle(0, 1, FINE)
    fine_cos, fine_sin = fine_cos * (1.0 / FREQ), fine_sin * (1.0 / FREQ)
    for i in range(local_bins // FINE):
        cc, cs = coarse_cos[i : i + 1], coarse_sin[i : i + 1]
        table[i * FINE : (i + 1) * FINE, :] = (cc * fine_cos - cs * fine_sin).astype(jnp.bfloat16)
        table[local_bins + i * FINE : local_bins + (i + 1) * FINE, :] = (
            -(cs * fine_cos + cc * fine_sin)
        ).astype(jnp.bfloat16)


def whiten_kernel(
    segments, bands, spectra_ref, first_ref, second_ref, bin_ref,
    rows, table, first_out, second_out, bin_out,
    near, window, edge_out, left_in, right_in, index_in, load_sem, send_sem, recv_sem,
):
    channels, local_bins = spectra_ref.shape[1:]
    groups = channels // REACH
    parts = 2 * local_bins // LANES
    half = parts // 2
    packed = REACH // 2
    seg, band = lax.axis_index("seg"), lax.axis_index("band")

    seg_there = {-1: seg > 0, 0: None, 1: seg < segments - 1}
    band_there = {-1: band > 0, 0: None, 1: band < bands - 1}
    peers = [(ds, db) for ds in (-1, 0, 1) for db in (-1, 0, 1) if (ds, db) != (0, 0)]

    def there(ds, db):
        if ds == 0:
            return band_there[db]
        if db == 0:
            return seg_there[ds]
        return jnp.logical_and(seg_there[ds], band_there[db])

    load = pltpu.make_async_copy(
        spectra_ref, near.at[:, pl.ds(REACH, channels), :], load_sem.at[0]
    )
    load.start()
    index_loads = [
        pltpu.make_async_copy(ref, index_in.at[k], load_sem.at[1 + k])
        for k, ref in enumerate((first_ref, second_ref, bin_ref))
    ]
    for index_load in index_loads:
        index_load.start()
    barrier = pltpu.get_barrier_semaphore()
    for ds, db in peers:
        @pl.when(there(ds, db))
        def _():
            pl.semaphore_signal(
                barrier, inc=1, device_id=(seg + ds, band + db), device_id_type=MESH
            )
    seg_span = 3 - jnp.where(seg == 0, 1, 0) - jnp.where(seg == segments - 1, 1, 0)
    band_span = 3 - jnp.where(band == 0, 1, 0) - jnp.where(band == bands - 1, 1, 0)
    pl.semaphore_wait(barrier, seg_span * band_span - 1)

    def sending(ds, db):
        slot = peers.index((ds, db))
        if db == 0:
            source = spectra_ref.at[:, pl.ds(channels - REACH if ds > 0 else 0, REACH), :]
            target = near.at[:, pl.ds(0 if ds > 0 else REACH + channels, REACH), :]
        else:
            side, box = (1, left_in) if db > 0 else (0, right_in)
            if ds == 0:
                source = edge_out.at[side]
                target = box.at[pl.ds(1, groups)]
            else:
                source = edge_out.at[side, pl.ds(groups - 1 if ds > 0 else 0, 1)]
                target = box.at[pl.ds(0 if ds > 0 else groups + 1, 1)]
        return pltpu.make_async_remote_copy(
            src_ref=source, dst_ref=target, send_sem=send_sem.at[slot],
            recv_sem=recv_sem.at[slot], device_id=(seg + ds, band + db), device_id_type=MESH,
        )

    def start(ds, db):
        @pl.when(there(ds, db))
        def _():
            sending(ds, db).start()

    def arrived(ds, db):
        @pl.when(there(-ds, -db))
        def _():
            sending(ds, db).wait_recv()

    start(-1, 0)
    start(1, 0)
    load.wait()

    lane = lax.broadcasted_iota(jnp.int32, (packed, LANES), 1)

    def edge(side, group):
        at = 0 if side == 0 else local_bins - LANES
        real = near[0, pl.ds(REACH + group * REACH, REACH), at : at + LANES].astype(jnp.float32)
        imag = near[1, pl.ds(REACH + group * REACH, REACH), at : at + LANES].astype(jnp.float32)
        power = real * real + imag * imag
        upper, lower = power[:packed], power[packed:]
        if side == 0:
            both = jnp.where(lane < HALF_WIN, upper, pltpu.roll(lower, HALF_WIN, 1))
        else:
            both = jnp.where(lane < HALF_WIN, pltpu.roll(upper, HALF_WIN, 1), lower)
        edge_out[side, group] = both.astype(jnp.bfloat16)

    for side, db in ((0, -1), (1, 1)):
        @pl.when(band_there[db])
        def _():
            for group in range(groups):
                edge(side, group)
        start(0, db)
        start(-1, db)
        start(1, db)
    for db, box in ((-1, left_in), (1, right_in)):
        @pl.when(jnp.logical_not(band_there[db]))
        def _():
            box[...] = jnp.zeros_like(box)

    shift = REACH - seg * channels
    for index_load in index_loads:
        index_load.wait()
    first_out[...] = (index_in[0] + shift) * parts
    second_out[...] = (index_in[1] + shift) * parts
    bin_out[...] = index_in[2] * parts
    distance = lax.broadcasted_iota(jnp.int32, (local_bins, local_bins), 0) - (
        lax.broadcasted_iota(jnp.int32, (local_bins, local_bins), 1)
    )
    window[...] = (jnp.abs(distance) <= HALF_WIN).astype(jnp.float32).astype(jnp.bfloat16)
    write_basis(band * local_bins, local_bins, table)

    source = lax.broadcasted_iota(jnp.int32, (LANES, LANES), 0)
    column = lax.broadcasted_iota(jnp.int32, (LANES, LANES), 1)

    def chosen(inside):
        return inside.astype(jnp.float32).astype(jnp.bfloat16)

    left_weights = [
        chosen((source < HALF_WIN) & (column <= source)),
        chosen((source >= HALF_WIN) & (column <= source - HALF_WIN)),
    ]
    right_weights = [
        chosen((source < HALF_WIN) & (column >= source + HALF_WIN)),
        chosen((source >= HALF_WIN) & (column >= source)),
    ]

    def dot(a, b):
        return jnp.dot(a, b, preferred_element_type=jnp.float32)

    def outside(box, group, weights):
        values = box[group]
        return jnp.concatenate([dot(values, weights[0]), dot(values, weights[1])], axis=0)

    def whiten(group):
        at = pl.ds(pl.multiple_of(group * REACH, REACH), REACH)
        real = near[0, at, :].astype(jnp.float32)
        imag = near[1, at, :].astype(jnp.float32)
        power = real * real + imag * imag
        high = power.astype(jnp.bfloat16)
        low = (power - high.astype(jnp.float32)).astype(jnp.bfloat16)
        total = dot(high, window[...]) + dot(low, window[...])
        for j in range(half):
            columns = slice(j * LANES, (j + 1) * LANES)
            piece = total[:, columns]
            if j == 0:
                piece = piece + outside(left_in, group, left_weights)
            if j == half - 1:
                piece = piece + outside(right_in, group, right_weights)
            scaling = lax.rsqrt(piece / (2 * HALF_WIN + 1) + epsilon)
            for k, part in ((0, real), (1, imag)):
                white = (part[:, columns] * scaling).astype(jnp.bfloat16).astype(jnp.float32)
                rows[pl.ds(group * (REACH * parts) + k * half + j, REACH, stride=parts), :] = white

    for db in (-1, 1):
        arrived(0, db)

    def local(group, carry):
        whiten(group)
        return carry

    lax.fori_loop(1, groups + 1, local, 0)
    for ds, group in ((1, 0), (-1, groups + 1)):
        arrived(ds, 0)
        arrived(ds, -1)
        arrived(ds, 1)

        @pl.when(seg_there[-ds])
        def _():
            whiten(group)
    for ds, db in peers:
        @pl.when(there(ds, db))
        def _():
            sending(ds, db).wait_send()


def pair_kernel(
    local_bins, bins, first_ref, second_ref, bin_ref, rows, table, out_ref, *banks
):
    parts = 2 * local_bins // LANES
    half = parts // 2
    for bank in banks:
        bank[...] = jnp.zeros_like(bank)

    upper = lax.broadcasted_iota(jnp.int32, (parts, LANES), 0) < half

    def group(step, carry):
        base = step * BANKS
        updates = []
        for k, bank in enumerate(banks):
            a = pl.multiple_of(first_ref[base + k], parts)
            b = pl.multiple_of(second_ref[base + k], parts)
            o = pl.multiple_of(bin_ref[base + k], parts)
            first = rows[pl.ds(a, parts), :]
            second = rows[pl.ds(b, parts), :]
            turned = pltpu.roll(second, half, 0)
            real = jnp.where(upper, second, turned)
            imag = jnp.where(upper, turned, -second)
            cross = first * real + pltpu.roll(first, half, 0) * imag
            updates.append((bank, o, bank[pl.ds(o, parts), :] + cross))
        for bank, o, updated in updates:
            bank[pl.ds(o, parts), :] = updated
        return carry

    lax.fori_loop(0, first_ref.shape[0] // BANKS, group, 0, unroll=4)

    lags = jnp.zeros((bins, LAGS), jnp.float32)
    for j in range(parts):
        piece = banks[0][pl.ds(j, bins, stride=parts), :]
        for bank in banks[1:]:
            piece = piece + bank[pl.ds(j, bins, stride=parts), :]
        high = piece.astype(jnp.bfloat16)
        low = (piece - high.astype(jnp.float32)).astype(jnp.bfloat16)
        basis = table[j * LANES : (j + 1) * LANES, :]
        lags += jnp.dot(high, basis, preferred_element_type=jnp.float32)
        lags += jnp.dot(low, basis, preferred_element_type=jnp.float32)
    out_ref[...] = lags


def sum_kernel(segments, bands, lags_ref, out_ref, send, near, mid, far, s1, r1, s2, r2):
    near_count = NEAR_SEGS * bands
    far_count = segments // NEAR_SEGS
    width = LAGS // bands
    seg, band = lax.axis_index("seg"), lax.axis_index("band")
    row, col = seg // NEAR_SEGS, seg % NEAR_SEGS
    me = col * bands + band

    def near_peer(d):
        p = lax.rem(me + d, near_count)
        return p, (row * NEAR_SEGS + p // bands, lax.rem(p, bands))

    def far_peer(d):
        p = lax.rem(row + d, far_count)
        return p, (p * NEAR_SEGS + col, band)

    barrier = pltpu.get_barrier_semaphore()
    for d in range(1, near_count):
        pl.semaphore_signal(barrier, inc=1, device_id=near_peer(d)[1], device_id_type=MESH)
    for d in range(1, far_count):
        pl.semaphore_signal(barrier, inc=1, device_id=far_peer(d)[1], device_id_type=MESH)
    for p in range(near_count):
        c, b = p // bands, p % bands
        block = [
            lags_ref[
                (r * NEAR_SEGS + c) * OB_DEV : (r * NEAR_SEGS + c + 1) * OB_DEV,
                b * width : (b + 1) * width,
            ]
            for r in range(far_count)
        ]
        send[p] = jnp.concatenate(block, axis=0).astype(jnp.bfloat16)
    pl.semaphore_wait(barrier, near_count - 1 + far_count - 1)

    def near_copy(d):
        p, device = near_peer(d)
        return pltpu.make_async_remote_copy(
            src_ref=send.at[p], dst_ref=near.at[d], send_sem=s1.at[d], recv_sem=r1.at[d],
            device_id=device, device_id_type=MESH,
        )

    def far_copy(d):
        p, device = far_peer(d)
        return pltpu.make_async_remote_copy(
            src_ref=mid.at[p], dst_ref=far.at[d], send_sem=s2.at[d], recv_sem=r2.at[d],
            device_id=device, device_id_type=MESH,
        )

    for d in range(1, near_count):
        near_copy(d).start()
    total = send[me].astype(jnp.float32)
    for d in range(1, near_count):
        near_copy(d).wait_recv()
        total += near[d].astype(jnp.float32)
    for r in range(far_count):
        mid[r] = total[r * OB_DEV : (r + 1) * OB_DEV]
    for d in range(1, far_count):
        far_copy(d).start()
    result = mid[row]
    for d in range(1, far_count):
        far_copy(d).wait_recv()
        result += far[d]
    out_ref[...] = result
    for d in range(1, near_count):
        near_copy(d).wait_send()
    for d in range(1, far_count):
        far_copy(d).wait_send()


def whiten(spectra, first, second, bins_at, segments, bands):
    _, channels, local_bins = spectra.shape
    parts = 2 * local_bins // LANES
    groups = channels // REACH
    count = first.shape[0]
    boxed = (count // LANES, LANES)
    vmem = pl.BlockSpec(memory_space=pltpu.VMEM)
    dma = pltpu.SemaphoreType.DMA
    edges = (groups + 2, REACH // 2, LANES)
    index = jax.ShapeDtypeStruct(boxed, jnp.int32)
    rows, table, *indices = pl.pallas_call(
        functools.partial(whiten_kernel, segments, bands),
        out_shape=[
            jax.ShapeDtypeStruct(((channels + 2 * REACH) * parts, LANES), jnp.float32),
            jax.ShapeDtypeStruct((2 * local_bins, LAGS), jnp.bfloat16),
            index, index, index,
        ],
        in_specs=[pl.BlockSpec(memory_space=pltpu.HBM)] * 4,
        out_specs=[vmem] * 5,
        scratch_shapes=[
            pltpu.VMEM((2, channels + 2 * REACH, local_bins), jnp.bfloat16),
            pltpu.VMEM((local_bins, local_bins), jnp.bfloat16),
            pltpu.VMEM((2, groups) + edges[1:], jnp.bfloat16),
            pltpu.VMEM(edges, jnp.bfloat16),
            pltpu.VMEM(edges, jnp.bfloat16),
            pltpu.VMEM((3,) + boxed, jnp.int32),
            dma((4,)), dma((8,)), dma((8,)),
        ],
        compiler_params=pltpu.CompilerParams(
            collective_id=0, has_side_effects=True, vmem_limit_bytes=32 * 2**20
        ),
        name="whiten",
    )(spectra, first.reshape(boxed), second.reshape(boxed), bins_at.reshape(boxed))
    return rows, table, [x.reshape(count) for x in indices]


def stack_pairs(rows, table, indices, local_bins, bins):
    parts = 2 * local_bins // LANES
    smem = pl.BlockSpec(memory_space=pltpu.SMEM)
    vmem = pl.BlockSpec(memory_space=pltpu.VMEM)
    return pl.pallas_call(
        functools.partial(pair_kernel, local_bins, bins),
        out_shape=jax.ShapeDtypeStruct((bins, LAGS), jnp.float32),
        in_specs=[smem, smem, smem, vmem, vmem],
        out_specs=vmem,
        scratch_shapes=[pltpu.VMEM((bins * parts, LANES), jnp.float32)] * BANKS,
        compiler_params=pltpu.CompilerParams(vmem_limit_bytes=32 * 2**20),
        name="pairs",
    )(*indices, rows, table)


def sum_lags(lags, segments, bands):
    near_count, far_count = NEAR_SEGS * bands, segments // NEAR_SEGS
    width = LAGS // bands
    vmem = pl.BlockSpec(memory_space=pltpu.VMEM)
    dma = pltpu.SemaphoreType.DMA
    return pl.pallas_call(
        functools.partial(sum_kernel, segments, bands),
        out_shape=jax.ShapeDtypeStruct((OB_DEV, width), jnp.float32),
        in_specs=[vmem],
        out_specs=vmem,
        scratch_shapes=[
            pltpu.VMEM((near_count, far_count * OB_DEV, width), jnp.bfloat16),
            pltpu.VMEM((near_count, far_count * OB_DEV, width), jnp.bfloat16),
            pltpu.VMEM((far_count, OB_DEV, width), jnp.float32),
            pltpu.VMEM((far_count, OB_DEV, width), jnp.float32),
            dma((near_count,)), dma((near_count,)), dma((far_count,)), dma((far_count,)),
        ],
        compiler_params=pltpu.CompilerParams(
            collective_id=1, has_side_effects=True, vmem_limit_bytes=32 * 2**20
        ),
        name="sums",
    )(lags)


def per_device(spectra, pair_first, pair_second, pair_bin):
    segments, bands = lax.axis_size("seg"), lax.axis_size("band")
    rows, table, indices = whiten(spectra, pair_first, pair_second, pair_bin, segments, bands)
    lags = stack_pairs(rows, table, indices, spectra.shape[2], segments * OB_DEV)
    return sum_lags(lags, segments, bands)


def solution(mesh):
    placed = (P(None, "seg", "band"), P("seg"), P("seg"), P("seg"))
    return jax.shard_map(
        per_device, mesh=mesh, in_specs=placed, out_specs=P("seg", "band"), check_vma=False
    )
```
